32 devices in a mesh: section: 2 (over x), col: 16 (over z, y, core).
Axes of the slice: x: 2, y: 2, z: 4, core: 2. Of those that a mesh axis runs over, the one named last changes fastest.
Arguments:
- rhs: float32 [16, 16384], P(None, ('section', 'col')), may hold values from -6 to 6
- inverse_blocks: float32 [128, 128, 128], P(('section', 'col')), may hold values from -1 to 1
- couplings: float32 [128, 2, 128, 128], P(('section', 'col')), may hold values from -0.25 to 0.25
- targets: int32 [128, 2], P(('section', 'col')), may hold values from 0 to 63, as said below
Outputs:
- forward_values: float32 [16, 16384], P(None, ('section', 'col'))
- solution: float32 [16, 16384], P(None, ('section', 'col'))
The draws below stay inside these ranges and needn't reach their ends.
Inputs may be any that keep to these rules, and one draw needn't show every extreme that they name: The value v = targets[j, k] names the block row with owner column v // 4 and local row v % 4 in the next section group; the 8 values in the rows of one device name 8 different owner columns. Rows of the last section group are not used.
All inputs are finite; a program needn't handle non-finite values.
Results may differ from the reference program's by a relative error of at most 0.0001.
Values sent between devices are 32-bit elements; how exact they have to be, the bound alone decides.
No kernel may reach another device: no remote copies, remote signals or barrier semaphores. Data moves between devices by JAX's collectives and lax.ppermute only.
A program may use at most 64 MiB of HBM per device.

```python
import math
import jax
import jax.numpy as jnp
from jax import lax

B = 128
LOC = 4
K = 2
NB = 128
RHS = 16
N = 16384
N_SECTION = 2
N_COL = 16


def draw_inverse_blocks(key, part):
    key = jax.random.fold_in(key, 11)
    first_key = jax.random.fold_in(key, 1)
    second_key = jax.random.fold_in(key, 2)
    diagonal_part = jax.random.uniform(first_key, (NB, B), jnp.float32, 0.6, 1.0)
    off_part = jnp.clip(jax.random.normal(second_key, (NB, B, B), jnp.float32), -4.0, 4.0) * (0.35 / math.sqrt(B))
    identity = jnp.eye(B, dtype=jnp.float32)
    return off_part * (1.0 - identity) + diagonal_part[:, :, None] * identity


def draw_targets(key, part):
    key = jax.random.fold_in(key, 23)
    device_keys = jax.random.split(jax.random.fold_in(key, 1), N_SECTION * N_COL)
    owners_all = jax.vmap(lambda single_key: jax.random.permutation(single_key, N_COL))(device_keys)
    owners_used = owners_all[:, :LOC * K].reshape(N_SECTION * N_COL * LOC, K).astype(jnp.int32)
    local_rows = jax.random.randint(jax.random.fold_in(key, 2), (N_SECTION * N_COL * LOC, K), 0, LOC, dtype=jnp.int32)
    return owners_used * LOC + local_rows


def steps_of(key, dims, pieces, least, high):
    level, own = 1.0, jax.random.fold_in(key, 6)
    for dim, parts in pieces:
        heights = jnp.exp(jax.random.uniform(jax.random.fold_in(own, dim), (parts,), jnp.float32, least / len(pieces), high / len(pieces)))
        level = level * jnp.repeat(heights, dims[dim] // parts).reshape([-1 if axis == dim else 1 for axis in range(len(dims))])
    return level


def centred(rng, dims, width, bound, cuts=(), kind=jnp.bfloat16):
    entries = jax.random.normal(rng, dims, jnp.float32) * width
    if len(cuts) > 0:
        entries = steps_of(rng, dims, cuts, -0.22, 0.18) * entries
    return jnp.clip(entries, min=-bound, max=bound).astype(kind)


def setup_inputs(seed: int = 0) -> dict:
    streams_of = jax.random.split(jax.random.key(seed), 5)
    return {
        "rhs": centred(streams_of[0], (RHS, N), 1.0, 6.0, ((1, 32),), jnp.float32),
        "inverse_blocks": draw_inverse_blocks(jax.random.fold_in(streams_of[4], 71), 0),
        "couplings": centred(streams_of[2], (NB, K, B, B), (2 * K * B) ** -0.5, 0.25, ((0, 32),), jnp.float32),
        "targets": draw_targets(jax.random.fold_in(streams_of[4], 71), 0),
    }


def reference(rhs, inverse_blocks, couplings, targets):
    precise = lax.Precision.HIGHEST
    sections = N_SECTION
    per_section = N_COL * LOC
    rhs_count = rhs.shape[0]
    values = rhs.reshape(rhs_count, sections, per_section, B).transpose(1, 2, 0, 3)
    inverses = inverse_blocks.reshape(sections, per_section, B, B)
    coupled = couplings.reshape(sections, per_section, K, B, B)
    aimed_rows = targets.reshape(sections, per_section, K).astype(jnp.int32)
    incoming = jnp.zeros((per_section, rhs_count, B), jnp.float32)
    forward_list = []
    for section_index in range(sections):
        solved = jnp.einsum("jrb,jbc->jrc", values[section_index] - incoming, inverses[section_index], precision=precise)
        forward_list.append(solved)
        if section_index + 1 < sections:
            products = jnp.einsum("jrb,jkbc->jkrc", solved, coupled[section_index], precision=precise)
            incoming = jax.ops.segment_sum(products.reshape(per_section * K, rhs_count, B), aimed_rows[section_index].reshape(-1), num_segments=per_section)
    back_terms = jnp.zeros((per_section, rhs_count, B), jnp.float32)
    backward_list = [None] * sections
    for section_index in range(sections - 1, -1, -1):
        solved = jnp.einsum("jrb,jcb->jrc", forward_list[section_index] - back_terms, inverses[section_index], precision=precise)
        backward_list[section_index] = solved
        if section_index > 0:
            picked = solved[aimed_rows[section_index - 1]]
            back_terms = jnp.einsum("jkrc,jkbc->jrb", picked, coupled[section_index - 1], precision=precise)
    forward_values = jnp.stack(forward_list).transpose(2, 0, 1, 3).reshape(rhs_count, -1)
    solution = jnp.stack(backward_list).transpose(2, 0, 1, 3).reshape(rhs_count, -1)
    return forward_values, solution
```

```python
import functools

import jax
import jax.numpy as jnp
from jax import lax
from jax.experimental import pallas as pl
from jax.experimental.pallas import tpu as pltpu
from jax.sharding import PartitionSpec as P

INDEX_ROWS = 8
VMEM = pl.BlockSpec(memory_space=pltpu.VMEM)
SMEM = pl.BlockSpec(memory_space=pltpu.SMEM)

precise = lax.Precision.HIGHEST


def times(left, right):
    return lax.dot_general(left, right, (((1,), (0,)), ((), ())), precision=precise)


def times_transposed(left, right):
    return lax.dot_general(left, right, (((1,), (1,)), ((), ())), precision=precise)


def kernel_call(kernel, out_shape, specs, name):
    return pl.pallas_call(
        kernel,
        out_shape=out_shape,
        in_specs=specs,
        out_specs=jax.tree.map(lambda _: VMEM, out_shape),
        compiler_params=pltpu.CompilerParams(vmem_limit_bytes=16 * 2**20),
        name=name,
    )


def summed_by_row(arrived_ref, local_count, rhs_count):
    sums = [None] * local_count
    for column in range(arrived_ref.shape[0]):
        block = arrived_ref[column, :rhs_count, :]
        row = arrived_ref[column, rhs_count : rhs_count + 1, :]
        for local in range(local_count):
            term = jnp.where(row == local, block, 0.0)
            sums[local] = term if sums[local] is None else sums[local] + term
    return sums


def place_answers(arrived_ref, answers_ref, solved, rhs_count):
    for column in range(arrived_ref.shape[0]):
        row = arrived_ref[column, rhs_count : rhs_count + 1, :]
        answer = jnp.zeros_like(solved[0])
        for local, values in enumerate(solved):
            answer = jnp.where(row == local, values, answer)
        answers_ref[column] = answer


def forward_kernel(targets_ref, rhs_ref, incoming_ref, inverse_ref, couplings_ref, values_ref, out_ref):
    local_count, width, _ = inverse_ref.shape
    fanout = couplings_ref.shape[1]
    rhs_count = rhs_ref.shape[0]
    out_ref[...] = jnp.full(out_ref.shape, -1.0, jnp.float32)
    for local in range(local_count):
        lanes = slice(local * width, (local + 1) * width)
        source = rhs_ref[:, lanes] - incoming_ref[:, lanes]
        solved = times(source, inverse_ref[local])
        values_ref[:, lanes] = solved
        for k in range(fanout):
            target = targets_ref[local, k]
            owner = target // local_count
            out_ref[owner, :rhs_count, :] = times(solved, couplings_ref[local, k])
            out_ref[owner, rhs_count:, :] = jnp.full(
                (out_ref.shape[1] - rhs_count, width), target % local_count, jnp.int32
            ).astype(jnp.float32)


def sum_kernel(arrived_ref, sums_ref):
    rhs_count, width = sums_ref.shape[0], arrived_ref.shape[2]
    local_count = sums_ref.shape[1] // width
    for local, total in enumerate(summed_by_row(arrived_ref, local_count, rhs_count)):
        sums_ref[:, local * width : (local + 1) * width] = total


def last_kernel(arrived_ref, rhs_ref, inverse_ref, pair_ref, answers_ref):
    local_count, width, _ = inverse_ref.shape
    rhs_count = rhs_ref.shape[0]
    sums = summed_by_row(arrived_ref, local_count, rhs_count)
    solved = []
    for local in range(local_count):
        lanes = slice(local * width, (local + 1) * width)
        forward = times(rhs_ref[:, lanes] - sums[local], inverse_ref[local])
        backward = times_transposed(forward, inverse_ref[local])
        pair_ref[0, :, lanes] = forward
        pair_ref[1, :, lanes] = backward
        solved.append(backward)
    place_answers(arrived_ref, answers_ref, solved, rhs_count)


def place_kernel(arrived_ref, solved_ref, answers_ref):
    rhs_count, width = solved_ref.shape[0], arrived_ref.shape[2]
    local_count = solved_ref.shape[1] // width
    solved = [solved_ref[:, i * width : (i + 1) * width] for i in range(local_count)]
    place_answers(arrived_ref, answers_ref, solved, rhs_count)


def backward_kernel(targets_ref, picked_ref, values_ref, inverse_ref, couplings_ref, solution_ref):
    local_count, width, _ = inverse_ref.shape
    for local in range(local_count):
        lanes = slice(local * width, (local + 1) * width)
        source = values_ref[:, lanes]
        for k in range(couplings_ref.shape[1]):
            owner = targets_ref[local, k] // local_count
            source = source - times_transposed(picked_ref[owner], couplings_ref[local, k])
        solution_ref[:, lanes] = times_transposed(source, inverse_ref[local])


def body(rhs, inverse_blocks, couplings, targets):
    sections = lax.axis_size("section")
    columns = lax.axis_size("col")
    my_section = lax.axis_index("section")
    local_count, width, _ = inverse_blocks.shape
    rhs_count = rhs.shape[0]
    up = [(s, (s + 1) % sections) for s in range(sections)]
    down = [(s, (s - 1) % sections) for s in range(sections)]
    flat = jax.ShapeDtypeStruct(rhs.shape, jnp.float32)
    slots = jax.ShapeDtypeStruct((columns, rhs_count + INDEX_ROWS, width), jnp.float32)
    answered = jax.ShapeDtypeStruct((columns, rhs_count, width), jnp.float32)
    pair = jax.ShapeDtypeStruct((2,) + rhs.shape, jnp.float32)

    def exchanged(value):
        return lax.all_to_all(value, "col", split_axis=0, concat_axis=0, tiled=True)

    next_inverse = lax.ppermute(inverse_blocks, "section", down)
    next_rhs = lax.ppermute(rhs, "section", down)

    incoming = jnp.zeros_like(rhs)
    for step in range(sections - 1):
        values, outgoing = kernel_call(
            forward_kernel, (flat, slots), [SMEM, VMEM, VMEM, VMEM, VMEM], "forward"
        )(targets, rhs, incoming, inverse_blocks, couplings)
        arrived = exchanged(outgoing)
        if step < sections - 2:
            sums = kernel_call(sum_kernel, flat, [VMEM], "sum_rows")(arrived)
            moved = lax.ppermute(sums, "section", up)
            incoming = jnp.where(my_section == 0, 0.0, moved)

    last, answers = kernel_call(last_kernel, (pair, answered), [VMEM, VMEM, VMEM], "last_section")(
        arrived, next_rhs, next_inverse
    )
    for step in range(sections - 1):
        picked = exchanged(answers)
        solved = kernel_call(
            backward_kernel, flat, [SMEM, VMEM, VMEM, VMEM, VMEM], "backward"
        )(targets, picked, values, inverse_blocks, couplings)
        if step < sections - 2:
            moved = lax.ppermute(solved, "section", down)
            following = jnp.where(my_section == sections - 2, last[1], moved)
            answers = kernel_call(place_kernel, answered, [VMEM, VMEM], "place")(arrived, following)

    final = lax.ppermute(last, "section", up)
    is_last = my_section == sections - 1
    return jnp.where(is_last, final[0], values), jnp.where(is_last, final[1], solved)


def solution(mesh):
    return jax.shard_map(
        body,
        mesh=mesh,
        in_specs=(
            P(None, ("section", "col")),
            P(("section", "col"), None, None),
            P(("section", "col"), None, None, None),
            P(("section", "col"), None),
        ),
        out_specs=(P(None, ("section", "col")), P(None, ("section", "col"))),
        check_vma=False,
    )
```

```python
import jax
import jax.numpy as jnp
from jax import lax
from jax.experimental import pallas as pl
from jax.experimental.pallas import tpu as pltpu
from jax.sharding import PartitionSpec as P

VMEM = pl.BlockSpec(memory_space=pltpu.VMEM)
COVER = 20_000_000_000
HBM = pl.BlockSpec(memory_space=pltpu.HBM)


def split(value):
    high = value.astype(jnp.bfloat16)
    return high, (value - high.astype(jnp.float32)).astype(jnp.bfloat16)


def times(left, right, contracted=0):
    rows = left.shape[0]
    left_high, left_low = split(left)
    right_high, right_low = right

    def dot(a, b):
        numbers = (((1,), (contracted,)), ((), ()))
        return lax.dot_general(a, b, numbers, preferred_element_type=jnp.float32)

    both = dot(jnp.concatenate([left_high, left_low], axis=0), right_high)
    return both[:rows] + (both[rows:] + dot(left_high, right_low))


def times_transposed(left, right):
    return times(left, right, 1)


def kernel_call(kernel, out_shape, specs, name, flops=None, scratch=(), vmem=16 * 2**20):
    cost = None
    if flops is not None:
        cost = pl.CostEstimate(flops=flops, bytes_accessed=0, transcendentals=0)
    return pl.pallas_call(
        kernel,
        out_shape=out_shape,
        in_specs=specs,
        out_specs=jax.tree.map(lambda _: VMEM, out_shape),
        compiler_params=pltpu.CompilerParams(vmem_limit_bytes=vmem),
        cost_estimate=cost,
        scratch_shapes=scratch,
        name=name,
    )


def split_kernel(*refs):
    count = len(refs) // 3
    for i in range(count):
        refs[count + 2 * i][...], refs[count + 2 * i + 1][...] = split(refs[i][...])


def split_arrays(arrays, flops):
    out = tuple(jax.ShapeDtypeStruct(a.shape, jnp.bfloat16) for a in arrays for _ in range(2))
    return kernel_call(split_kernel, out, [VMEM] * len(arrays), "split_weights", flops)(*arrays)


def lane_blocks(width, count):
    return [slice(i * width, (i + 1) * width) for i in range(count)]


def summed_by_row(arrived_ref, local_count, rhs_count):
    stride = rhs_count + 1
    sums = [None] * local_count
    for start in range(0, arrived_ref.shape[0], stride):
        block = arrived_ref[start : start + rhs_count, :]
        row = arrived_ref[start + rhs_count : start + stride, :]
        for local in range(local_count):
            term = jnp.where(row == local, block, 0.0)
            sums[local] = term if sums[local] is None else sums[local] + term
    return sums


def place_answers(arrived_ref, answers_ref, solved, rhs_count):
    stride = rhs_count + 1
    for column in range(answers_ref.shape[0]):
        last = (column + 1) * stride
        row = arrived_ref[last - 1 : last, :]
        answer = jnp.zeros_like(solved[0])
        for local, values in enumerate(solved):
            answer = jnp.where(row == local, values, answer)
        answers_ref[column] = answer


def forward_kernel(targets_hbm, rhs_hbm, inverse_hbm, couplings_hbm, *rest):
    *incoming_ref, values_ref, passed_ref, owners_ref, out_ref = rest[:-5]
    targets_ref, rhs_ref, inverse_ref, couplings_ref, sems = rest[-5:]
    sources = (targets_hbm, rhs_hbm, inverse_hbm, couplings_hbm)
    places = (targets_ref, rhs_ref, inverse_ref, couplings_ref)
    copies = [
        pltpu.make_async_copy(source, place, sems.at[i])
        for i, (source, place) in enumerate(zip(sources, places))
    ]
    for copy in copies:
        copy.start()
    out_ref[...] = jnp.full(out_ref.shape, -1.0, jnp.float32)
    local_count, width, _ = inverse_ref.shape
    fanout = couplings_ref.shape[1]
    rhs_count = rhs_ref.shape[0]
    stride = rhs_count + 1
    copies[1].wait()
    copies[2].wait()
    passed_ref[...] = rhs_ref[...]
    solved = []
    for local, lanes in enumerate(lane_blocks(width, local_count)):
        source = rhs_ref[:, lanes]
        if incoming_ref:
            source = source - incoming_ref[0][:, lanes]
        solved.append(times(source, split(inverse_ref[local])))
        values_ref[:, lanes] = solved[local]
    copies[0].wait()
    copies[3].wait()
    for local in range(local_count):
        for k in range(fanout):
            target = targets_ref[k, local]
            owner = target // local_count
            start = owner * stride
            row = jnp.full((1, width), target % local_count, jnp.int32)
            out_ref[pl.ds(start, rhs_count), :] = times(solved[local], split(couplings_ref[local, k]))
            out_ref[pl.ds(start + rhs_count, 1), :] = row.astype(jnp.float32)
            pair = local * fanout + k
            owners_ref[pair : pair + 1, :] = jnp.full((1, width), owner, jnp.int32)


def sum_kernel(arrived_ref, sums_ref):
    rhs_count, width = sums_ref.shape[0], arrived_ref.shape[1]
    lanes = lane_blocks(width, sums_ref.shape[1] // width)
    for local, total in enumerate(summed_by_row(arrived_ref, len(lanes), rhs_count)):
        sums_ref[:, lanes[local]] = total


def last_kernel(arrived_ref, rhs_ref, high_ref, low_ref, pair_ref, answers_ref):
    local_count, width, _ = high_ref.shape
    rhs_count = rhs_ref.shape[0]
    sums = summed_by_row(arrived_ref, local_count, rhs_count)
    lanes = lane_blocks(width, local_count)
    inverse = [(high_ref[i], low_ref[i]) for i in range(local_count)]
    forward = [times(rhs_ref[:, lanes[i]] - sums[i], inverse[i]) for i in range(local_count)]
    backward = [times_transposed(forward[i], inverse[i]) for i in range(local_count)]
    for local in range(local_count):
        pair_ref[0, :, lanes[local]] = forward[local]
        pair_ref[1, :, lanes[local]] = backward[local]
    place_answers(arrived_ref, answers_ref, backward, rhs_count)


def place_kernel(arrived_ref, solved_ref, answers_ref):
    rhs_count, width = solved_ref.shape[0], arrived_ref.shape[1]
    lanes = lane_blocks(width, solved_ref.shape[1] // width)
    place_answers(arrived_ref, answers_ref, [solved_ref[:, lane] for lane in lanes], rhs_count)


def backward_kernel(
    owners_ref,
    picked_ref,
    values_ref,
    inverse_high_ref,
    inverse_low_ref,
    couplings_high_ref,
    couplings_low_ref,
    *rest,
):
    *pair_ref, solution_ref = rest
    if pair_ref:
        pair_ref, forward_ref = pair_ref
    local_count, width, _ = inverse_high_ref.shape
    fanout = couplings_high_ref.shape[1]
    lanes = lane_blocks(width, local_count)

    def solve():
        blocks = [jnp.zeros(picked_ref.shape[1:], jnp.float32)] * (local_count * fanout)
        for column in range(picked_ref.shape[0]):
            block = picked_ref[column]
            for pair in range(local_count * fanout):
                chosen = owners_ref[pair : pair + 1, :] == column
                blocks[pair] = jnp.where(chosen, block, blocks[pair])
        sources = []
        for local in range(local_count):
            source = values_ref[:, lanes[local]]
            for k in range(fanout):
                coupling = (couplings_high_ref[local, k], couplings_low_ref[local, k])
                source = source - times_transposed(blocks[local * fanout + k], coupling)
            sources.append(source)
        for local in range(local_count):
            inverse = (inverse_high_ref[local], inverse_low_ref[local])
            solution_ref[:, lanes[local]] = times_transposed(sources[local], inverse)

    if not isinstance(pair_ref, list):
        is_last = lax.axis_index("section") == lax.axis_size("section") - 1

        @pl.when(is_last)
        def _():
            forward_ref[...] = pair_ref[0]
            solution_ref[...] = pair_ref[1]

        @pl.when(jnp.logical_not(is_last))
        def _():
            forward_ref[...] = values_ref[...]
            solve()

    else:
        solve()


def body(rhs, inverse_blocks, couplings, targets):
    sections = lax.axis_size("section")
    columns = lax.axis_size("col")
    my_section = lax.axis_index("section")
    local_count, width, _ = inverse_blocks.shape
    rhs_count = rhs.shape[0]
    stride = rhs_count + 1
    up = [(s, (s + 1) % sections) for s in range(sections)]
    down = [(s, (s - 1) % sections) for s in range(sections)]
    flat = jax.ShapeDtypeStruct(rhs.shape, jnp.float32)
    slots = jax.ShapeDtypeStruct((columns * stride, width), jnp.float32)
    answered = jax.ShapeDtypeStruct((columns, rhs_count, width), jnp.float32)
    pair = jax.ShapeDtypeStruct((2,) + rhs.shape, jnp.float32)
    owners = jax.ShapeDtypeStruct((local_count * couplings.shape[1], width), jnp.int32)
    aimed = targets.T
    inputs = (aimed, rhs, inverse_blocks, couplings)
    held = [pltpu.SMEM(aimed.shape, jnp.int32)]
    held += [pltpu.VMEM(a.shape, a.dtype) for a in inputs[1:]]
    held += [pltpu.SemaphoreType.DMA((len(inputs),))]

    def exchanged(value):
        return lax.all_to_all(value, "col", split_axis=0, concat_axis=0, tiled=True)

    next_inverse = lax.ppermute(inverse_blocks, "section", down)

    incoming = ()
    for step in range(sections - 1):
        values, passed, owner_rows, outgoing = kernel_call(
            forward_kernel,
            (flat, flat, owners, slots),
            [HBM] * len(inputs) + [VMEM] * len(incoming),
            "forward",
            scratch=held,
            vmem=60*2**20,
        )(*inputs, *incoming)
        arrived = exchanged(outgoing.reshape(columns, stride, 1, width)).reshape(slots.shape)
        if step < sections - 2:
            sums = kernel_call(sum_kernel, flat, [VMEM], "sum_rows")(arrived)
            moved = lax.ppermute(sums, "section", up)
            incoming = (jnp.where(my_section == 0, 0.0, moved),)

    next_rhs = lax.ppermute(passed, "section", down)
    next_split = split_arrays((next_inverse,), COVER)
    weights = split_arrays((inverse_blocks, couplings), COVER)
    last, answers = kernel_call(last_kernel, (pair, answered), [VMEM] * 4, "last_section")(
        arrived, next_rhs, *next_split
    )
    for step in range(sections - 1):
        picked = exchanged(answers)
        operands = (owner_rows, picked, values, *weights)
        if step < sections - 2:
            solved = kernel_call(backward_kernel, flat, [VMEM] * len(operands), "backward")(
                *operands
            )
            moved = lax.ppermute(solved, "section", down)
            following = jnp.where(my_section == sections - 2, last[1], moved)
            answers = kernel_call(place_kernel, answered, [VMEM, VMEM], "place")(arrived, following)

    final = lax.ppermute(last, "section", up)
    return kernel_call(backward_kernel, (flat, flat), [VMEM] * (len(operands) + 1), "backward_last")(
        *operands, final
    )


def solution(mesh):
    return jax.shard_map(
        body,
        mesh=mesh,
        in_specs=(
            P(None, ("section", "col")),
            P(("section", "col"), None, None),
            P(("section", "col"), None, None, None),
            P(("section", "col"), None),
        ),
        out_specs=(P(None, ("section", "col")), P(None, ("section", "col"))),
        check_vma=False,
    )
```

```python
import functools

import jax
import jax.numpy as jnp
from jax import lax
from jax.experimental import pallas as pl
from jax.experimental.pallas import tpu as pltpu
from jax.sharding import PartitionSpec as P

VMEM = pl.BlockSpec(memory_space=pltpu.VMEM)
COVER = 20_000_000_000
HBM = pl.BlockSpec(memory_space=pltpu.HBM)


def split(value):
    high = value.astype(jnp.bfloat16)
    return high, (value - high.astype(jnp.float32)).astype(jnp.bfloat16)


def times(left, right, contracted=0):
    rows = left.shape[0]
    left_high, left_low = split(left)
    right_high, right_low = right

    def dot(a, b):
        numbers = (((1,), (contracted,)), ((), ()))
        return lax.dot_general(a, b, numbers, preferred_element_type=jnp.float32)

    both = dot(jnp.concatenate([left_high, left_low], axis=0), right_high)
    return both[:rows] + (both[rows:] + dot(left_high, right_low))


def times_transposed(left, right):
    return times(left, right, 1)


def kernel_call(kernel, out_shape, specs, name, flops=None, scratch=(), vmem=16 * 2**20):
    cost = None
    if flops is not None:
        cost = pl.CostEstimate(flops=flops, bytes_accessed=0, transcendentals=0)
    return pl.pallas_call(
        kernel,
        out_shape=out_shape,
        in_specs=specs,
        out_specs=jax.tree.map(lambda _: VMEM, out_shape),
        compiler_params=pltpu.CompilerParams(vmem_limit_bytes=vmem),
        cost_estimate=cost,
        scratch_shapes=scratch,
        name=name,
    )


def split_kernel(count, kept, *refs):
    passed, arrays, refs = refs[:kept], refs[kept : kept + count], refs[kept + count :]
    for i in range(kept):
        refs[i][...] = passed[i][...]
    for i, array in enumerate(arrays):
        at = kept + 2 * i
        refs[at][...], refs[at + 1][...] = split(array[...])


def split_arrays(arrays, flops, kept=()):
    out = tuple(jax.ShapeDtypeStruct(a.shape, a.dtype) for a in kept)
    out += tuple(jax.ShapeDtypeStruct(a.shape, jnp.bfloat16) for a in arrays for _ in range(2))
    kernel = functools.partial(split_kernel, len(arrays), len(kept))
    specs = [VMEM] * (len(kept) + len(arrays))
    return kernel_call(kernel, out, specs, "split_weights", flops)(*kept, *arrays)


def lane_blocks(width, count):
    return [slice(i * width, (i + 1) * width) for i in range(count)]


def summed_by_row(arrived_ref, local_count, rhs_count):
    stride = rhs_count + 1
    sums = [None] * local_count
    for start in range(0, arrived_ref.shape[0], stride):
        block = arrived_ref[start : start + rhs_count, :]
        row = arrived_ref[start + rhs_count : start + stride, :]
        for local in range(local_count):
            term = jnp.where(row == local, block, 0.0)
            sums[local] = term if sums[local] is None else sums[local] + term
    return sums


def place_answers(arrived_ref, answers_ref, solved, rhs_count):
    stride = rhs_count + 1
    for column in range(answers_ref.shape[0]):
        last = (column + 1) * stride
        row = arrived_ref[last - 1 : last, :]
        answer = jnp.zeros_like(solved[0])
        for local, values in enumerate(solved):
            answer = jnp.where(row == local, values, answer)
        answers_ref[column] = answer


def forward_kernel(targets_hbm, rhs_hbm, inverse_hbm, couplings_hbm, *rest):
    *incoming_ref, values_ref, passed_ref, slots_ref, out_ref = rest[:-5]
    targets_ref, rhs_ref, inverse_ref, couplings_ref, sems = rest[-5:]
    sources = (targets_hbm, rhs_hbm, inverse_hbm, couplings_hbm)
    places = (targets_ref, rhs_ref, inverse_ref, couplings_ref)
    copies = [
        pltpu.make_async_copy(source, place, sems.at[i])
        for i, (source, place) in enumerate(zip(sources, places))
    ]
    for copy in copies:
        copy.start()
    out_ref[...] = jnp.full(out_ref.shape, -1.0, jnp.float32)
    local_count, width, _ = inverse_ref.shape
    fanout = couplings_ref.shape[1]
    rhs_count = rhs_ref.shape[0]
    stride = rhs_count + 1
    columns = out_ref.shape[0] // stride
    copies[1].wait()
    copies[2].wait()
    passed_ref[...] = rhs_ref[...]
    solved = []
    for local, lanes in enumerate(lane_blocks(width, local_count)):
        source = rhs_ref[:, lanes]
        if incoming_ref:
            source = source - incoming_ref[0][:, lanes]
        solved.append(times(source, split(inverse_ref[local])))
        values_ref[:, lanes] = solved[local]
    copies[0].wait()
    copies[3].wait()
    for local in range(local_count):
        for k in range(fanout):
            target = targets_ref[k, local]
            slot = columns - 1 - target // local_count
            start = slot * stride
            row = jnp.full((1, width), target % local_count, jnp.int32)
            out_ref[pl.ds(start, rhs_count), :] = times(solved[local], split(couplings_ref[local, k]))
            out_ref[pl.ds(start + rhs_count, 1), :] = row.astype(jnp.float32)
            pair = local * fanout + k
            slots_ref[pair : pair + 1, :] = jnp.full((1, width), slot, jnp.int32)


def sum_kernel(arrived_ref, sums_ref):
    rhs_count, width = sums_ref.shape[0], arrived_ref.shape[1]
    lanes = lane_blocks(width, sums_ref.shape[1] // width)
    for local, total in enumerate(summed_by_row(arrived_ref, len(lanes), rhs_count)):
        sums_ref[:, lanes[local]] = total


def last_kernel(arrived_ref, rhs_ref, high_ref, low_ref, pair_ref, answers_ref):
    local_count, width, _ = high_ref.shape
    rhs_count = rhs_ref.shape[0]
    sums = summed_by_row(arrived_ref, local_count, rhs_count)
    lanes = lane_blocks(width, local_count)
    inverse = [(high_ref[i], low_ref[i]) for i in range(local_count)]
    forward = [times(rhs_ref[:, lanes[i]] - sums[i], inverse[i]) for i in range(local_count)]
    backward = [times_transposed(forward[i], inverse[i]) for i in range(local_count)]
    for local in range(local_count):
        pair_ref[0, :, lanes[local]] = forward[local]
        pair_ref[1, :, lanes[local]] = backward[local]
    place_answers(arrived_ref, answers_ref, backward, rhs_count)


def place_kernel(arrived_ref, solved_ref, answers_ref):
    rhs_count, width = solved_ref.shape[0], arrived_ref.shape[1]
    lanes = lane_blocks(width, solved_ref.shape[1] // width)
    place_answers(arrived_ref, answers_ref, [solved_ref[:, lane] for lane in lanes], rhs_count)


def backward_kernel(
    slots_ref,
    picked_ref,
    values_ref,
    inverse_high_ref,
    inverse_low_ref,
    couplings_high_ref,
    couplings_low_ref,
    *rest,
):
    *pair_ref, solution_ref = rest
    if pair_ref:
        pair_ref, forward_ref = pair_ref
    local_count, width, _ = inverse_high_ref.shape
    fanout = couplings_high_ref.shape[1]
    lanes = lane_blocks(width, local_count)

    def solve():
        blocks = [jnp.zeros(picked_ref.shape[1:], jnp.float32)] * (local_count * fanout)
        for column in range(picked_ref.shape[0]):
            block = picked_ref[column]
            for pair in range(local_count * fanout):
                chosen = slots_ref[pair : pair + 1, :] == column
                blocks[pair] = jnp.where(chosen, block, blocks[pair])
        sources = []
        for local in range(local_count):
            source = values_ref[:, lanes[local]]
            for k in range(fanout):
                coupling = (couplings_high_ref[local, k], couplings_low_ref[local, k])
                source = source - times_transposed(blocks[local * fanout + k], coupling)
            sources.append(source)
        for local in range(local_count):
            inverse = (inverse_high_ref[local], inverse_low_ref[local])
            solution_ref[:, lanes[local]] = times_transposed(sources[local], inverse)

    if not isinstance(pair_ref, list):
        is_last = lax.axis_index("section") == lax.axis_size("section") - 1

        @pl.when(is_last)
        def _():
            forward_ref[...] = pair_ref[0]
            solution_ref[...] = pair_ref[1]

        @pl.when(jnp.logical_not(is_last))
        def _():
            forward_ref[...] = values_ref[...]
            solve()

    else:
        solve()


def body(rhs, inverse_blocks, couplings, targets):
    sections = lax.axis_size("section")
    columns = lax.axis_size("col")
    my_section = lax.axis_index("section")
    local_count, width, _ = inverse_blocks.shape
    rhs_count = rhs.shape[0]
    stride = rhs_count + 1
    up = [(s, (s + 1) % sections) for s in range(sections)]
    down = [(s, (s - 1) % sections) for s in range(sections)]
    flat = jax.ShapeDtypeStruct(rhs.shape, jnp.float32)
    slots = jax.ShapeDtypeStruct((columns * stride, width), jnp.float32)
    answered = jax.ShapeDtypeStruct((columns, rhs_count, width), jnp.float32)
    pair = jax.ShapeDtypeStruct((2,) + rhs.shape, jnp.float32)
    owners = jax.ShapeDtypeStruct((local_count * couplings.shape[1], width), jnp.int32)
    aimed = targets.T
    inputs = (aimed, rhs, inverse_blocks, couplings)
    held = [pltpu.SMEM(aimed.shape, jnp.int32)]
    held += [pltpu.VMEM(a.shape, a.dtype) for a in inputs[1:]]
    held += [pltpu.SemaphoreType.DMA((len(inputs),))]

    members = [list(range(columns))[::-1]]

    def exchanged(value):
        return lax.all_to_all(
            value, "col", split_axis=0, concat_axis=0, tiled=True, axis_index_groups=members
        )

    next_inverse = lax.ppermute(inverse_blocks, "section", down)

    incoming = ()
    for step in range(sections - 1):
        values, passed, slot_rows, outgoing = kernel_call(
            forward_kernel,
            (flat, flat, owners, slots),
            [HBM] * len(inputs) + [VMEM] * len(incoming),
            "forward",
            scratch=held,
            vmem=60*2**20,
        )(*inputs, *incoming)
        arrived = exchanged(outgoing.reshape(columns, stride, 1, width)).reshape(slots.shape)
        if step < sections - 2:
            sums = kernel_call(sum_kernel, flat, [VMEM], "sum_rows")(arrived)
            moved = lax.ppermute(sums, "section", up)
            incoming = (jnp.where(my_section == 0, 0.0, moved),)

    next_rhs = lax.ppermute(passed, "section", down)
    next_split = split_arrays((next_inverse,), COVER)
    slot_rows, values, *weights = split_arrays(
        (inverse_blocks, couplings), COVER, (slot_rows, values)
    )
    last, answers = kernel_call(last_kernel, (pair, answered), [VMEM] * 4, "last_section")(
        arrived, next_rhs, *next_split
    )
    for step in range(sections - 1):
        picked = exchanged(answers)
        operands = (slot_rows, picked, values, *weights)
        if step < sections - 2:
            solved = kernel_call(backward_kernel, flat, [VMEM] * len(operands), "backward")(
                *operands
            )
            moved = lax.ppermute(solved, "section", down)
            following = jnp.where(my_section == sections - 2, last[1], moved)
            answers = kernel_call(place_kernel, answered, [VMEM, VMEM], "place")(arrived, following)

    final = lax.ppermute(last, "section", up)
    return kernel_call(backward_kernel, (flat, flat), [VMEM] * (len(operands) + 1), "backward_last")(
        *operands, final
    )


def solution(mesh):
    return jax.shard_map(
        body,
        mesh=mesh,
        in_specs=(
            P(None, ("section", "col")),
            P(("section", "col"), None, None),
            P(("section", "col"), None, None, None),
            P(("section", "col"), None),
        ),
        out_specs=(P(None, ("section", "col")), P(None, ("section", "col"))),
        check_vma=False,
    )
```

```python
import functools

import jax
import jax.numpy as jnp
from jax import lax
from jax.experimental import pallas as pl
from jax.experimental.pallas import tpu as pltpu
from jax.sharding import PartitionSpec as P

VMEM = pl.BlockSpec(memory_space=pltpu.VMEM)
FIRST = 7
SECOND = 11
COVER = 20_000_000_000
HBM = pl.BlockSpec(memory_space=pltpu.HBM)


def split(value):
    high = value.astype(jnp.bfloat16)
    return high, (value - high.astype(jnp.float32)).astype(jnp.bfloat16)


def times(left, right, contracted=0):
    rows = left.shape[0]
    left_high, left_low = split(left)
    right_high, right_low = right

    def dot(a, b):
        numbers = (((1,), (contracted,)), ((), ()))
        return lax.dot_general(a, b, numbers, preferred_element_type=jnp.float32)

    both = dot(jnp.concatenate([left_high, left_low], axis=0), right_high)
    return both[:rows] + (both[rows:] + dot(left_high, right_low))


def times_transposed(left, right):
    return times(left, right, 1)


def kernel_call(kernel, out_shape, specs, name, flops=None, scratch=(), vmem=16 * 2**20):
    cost = None
    if flops is not None:
        cost = pl.CostEstimate(flops=flops, bytes_accessed=0, transcendentals=0)
    return pl.pallas_call(
        kernel,
        out_shape=out_shape,
        in_specs=specs,
        out_specs=jax.tree.map(lambda _: VMEM, out_shape),
        compiler_params=pltpu.CompilerParams(vmem_limit_bytes=vmem),
        cost_estimate=cost,
        scratch_shapes=scratch,
        name=name,
    )


def split_kernel(count, kept, *refs):
    passed, arrays, refs = refs[:kept], refs[kept : kept + count], refs[kept + count :]
    for i in range(kept):
        refs[i][...] = passed[i][...]
    for i, array in enumerate(arrays):
        at = kept + 2 * i
        refs[at][...], refs[at + 1][...] = split(array[...])


def split_arrays(arrays, flops, kept=()):
    out = tuple(jax.ShapeDtypeStruct(a.shape, a.dtype) for a in kept)
    out += tuple(jax.ShapeDtypeStruct(a.shape, jnp.bfloat16) for a in arrays for _ in range(2))
    kernel = functools.partial(split_kernel, len(arrays), len(kept))
    specs = [VMEM] * (len(kept) + len(arrays))
    return kernel_call(kernel, out, specs, "split_weights", flops)(*kept, *arrays)


def lane_blocks(width, count):
    return [slice(i * width, (i + 1) * width) for i in range(count)]


def summed_by_row(arrived_ref, local_count, rhs_count):
    stride = rhs_count + 1
    sums = [None] * local_count
    for start in range(0, arrived_ref.shape[0], stride):
        block = arrived_ref[start : start + rhs_count, :]
        row = arrived_ref[start + rhs_count : start + stride, :]
        for local in range(local_count):
            term = jnp.where(row == local, block, 0.0)
            sums[local] = term if sums[local] is None else sums[local] + term
    return sums


def place_answers(arrived_ref, answers_ref, solved, rhs_count):
    stride = rhs_count + 1
    columns = answers_ref.shape[0]
    for column in range(columns):
        last = ((column ^ (FIRST % columns)) + 1) * stride
        row = arrived_ref[last - 1 : last, :]
        answer = jnp.zeros_like(solved[0])
        for local, values in enumerate(solved):
            answer = jnp.where(row == local, values, answer)
        answers_ref[column ^ (SECOND % columns)] = answer


def forward_kernel(targets_hbm, rhs_hbm, inverse_hbm, couplings_hbm, *rest):
    *incoming_ref, values_ref, slots_ref, out_ref = rest[:-5]
    targets_ref, rhs_ref, inverse_ref, couplings_ref, sems = rest[-5:]
    local_count, width, _ = inverse_ref.shape
    fanout = couplings_ref.shape[1]
    rhs_count = rhs_ref.shape[0]
    stride = rhs_count + 1
    columns = out_ref.shape[0] // stride
    has_targets = lax.axis_index("section") < lax.axis_size("section") - 1

    @pl.when(has_targets)
    def _():
        sources = (targets_hbm, rhs_hbm, inverse_hbm, couplings_hbm)
        places = (targets_ref, rhs_ref, inverse_ref, couplings_ref)
        copies = [
            pltpu.make_async_copy(source, place, sems.at[i])
            for i, (source, place) in enumerate(zip(sources, places))
        ]
        for copy in copies:
            copy.start()
        out_ref[...] = jnp.full(out_ref.shape, -1.0, jnp.float32)
        copies[1].wait()
        copies[2].wait()
        solved = []
        for local, lanes in enumerate(lane_blocks(width, local_count)):
            source = rhs_ref[:, lanes]
            if incoming_ref:
                source = source - incoming_ref[0][:, lanes]
            solved.append(times(source, split(inverse_ref[local])))
            values_ref[:, lanes] = solved[local]
        copies[0].wait()
        copies[3].wait()
        for local in range(local_count):
            for k in range(fanout):
                target = targets_ref[k, local]
                owner = target // local_count
                start = (owner ^ (FIRST % columns)) * stride
                product = times(solved[local], split(couplings_ref[local, k]))
                row = jnp.full((1, width), target % local_count, jnp.int32)
                out_ref[pl.ds(start, rhs_count), :] = product
                out_ref[pl.ds(start + rhs_count, 1), :] = row.astype(jnp.float32)
                slot = jnp.full((1, width), owner ^ (SECOND % columns), jnp.int32)
                pair = local * fanout + k
                slots_ref[pair : pair + 1, :] = slot

    @pl.when(jnp.logical_not(has_targets))
    def _():
        out_ref[...] = jnp.full(out_ref.shape, -1.0, jnp.float32)
        values_ref[...] = jnp.zeros(values_ref.shape, jnp.float32)
        slots_ref[...] = jnp.zeros(slots_ref.shape, jnp.int32)


def sum_kernel(arrived_ref, sums_ref):
    rhs_count, width = sums_ref.shape[0], arrived_ref.shape[1]
    lanes = lane_blocks(width, sums_ref.shape[1] // width)
    for local, total in enumerate(summed_by_row(arrived_ref, len(lanes), rhs_count)):
        sums_ref[:, lanes[local]] = total


def solve_last(rhs_ref, sums, high_ref, low_ref):
    local_count, width, _ = high_ref.shape
    lanes = lane_blocks(width, local_count)
    inverse = [(high_ref[i], low_ref[i]) for i in range(local_count)]
    forward = [times(rhs_ref[:, lanes[i]] - sums[i], inverse[i]) for i in range(local_count)]
    return forward, [times_transposed(forward[i], inverse[i]) for i in range(local_count)]


def last_kernel(arrived_ref, rhs_ref, high_ref, low_ref, sums_ref, *rest):
    *solved_ref, answers_ref = rest
    local_count, width, _ = high_ref.shape
    rhs_count = rhs_ref.shape[0]
    sums = summed_by_row(arrived_ref, local_count, rhs_count)
    for local, lanes in enumerate(lane_blocks(width, local_count)):
        sums_ref[:, lanes] = sums[local]
    _, backward = solve_last(rhs_ref, sums, high_ref, low_ref)
    for ref in solved_ref:
        for local, lanes in enumerate(lane_blocks(width, local_count)):
            ref[:, lanes] = backward[local]
    place_answers(arrived_ref, answers_ref, backward, rhs_count)


def place_kernel(arrived_ref, solved_ref, answers_ref):
    rhs_count, width = solved_ref.shape[0], arrived_ref.shape[1]
    lanes = lane_blocks(width, solved_ref.shape[1] // width)
    place_answers(arrived_ref, answers_ref, [solved_ref[:, lane] for lane in lanes], rhs_count)


def backward_kernel(
    slots_ref,
    picked_ref,
    values_ref,
    inverse_high_ref,
    inverse_low_ref,
    couplings_high_ref,
    couplings_low_ref,
    *rest,
):
    *last_refs, solution_ref = rest
    local_count, width, _ = inverse_high_ref.shape
    fanout = couplings_high_ref.shape[1]
    lanes = lane_blocks(width, local_count)

    def solve():
        blocks = [jnp.zeros(picked_ref.shape[1:], jnp.float32)] * (local_count * fanout)
        for column in range(picked_ref.shape[0]):
            block = picked_ref[column]
            for pair in range(local_count * fanout):
                chosen = slots_ref[pair : pair + 1, :] == column
                blocks[pair] = jnp.where(chosen, block, blocks[pair])
        sources = []
        for local in range(local_count):
            source = values_ref[:, lanes[local]]
            for k in range(fanout):
                coupling = (couplings_high_ref[local, k], couplings_low_ref[local, k])
                source = source - times_transposed(blocks[local * fanout + k], coupling)
            sources.append(source)
        for local in range(local_count):
            inverse = (inverse_high_ref[local], inverse_low_ref[local])
            solution_ref[:, lanes[local]] = times_transposed(sources[local], inverse)

    if last_refs:
        rhs_ref, sums_ref, forward_ref = last_refs
        is_last = lax.axis_index("section") == lax.axis_size("section") - 1

        @pl.when(is_last)
        def _():
            sums = [sums_ref[:, lane] for lane in lanes]
            results = solve_last(rhs_ref, sums, inverse_high_ref, inverse_low_ref)
            for local, lane in enumerate(lanes):
                forward_ref[:, lane] = results[0][local]
                solution_ref[:, lane] = results[1][local]

        @pl.when(jnp.logical_not(is_last))
        def _():
            forward_ref[...] = values_ref[...]
            solve()

    else:
        solve()


def body(rhs, inverse_blocks, couplings, targets):
    sections = lax.axis_size("section")
    columns = lax.axis_size("col")
    my_section = lax.axis_index("section")
    local_count, width, _ = inverse_blocks.shape
    rhs_count = rhs.shape[0]
    stride = rhs_count + 1
    up = [(s, (s + 1) % sections) for s in range(sections)]
    down = [(s, (s - 1) % sections) for s in range(sections)]
    flat = jax.ShapeDtypeStruct(rhs.shape, jnp.float32)
    slots = jax.ShapeDtypeStruct((columns * stride, width), jnp.float32)
    answered = jax.ShapeDtypeStruct((columns, rhs_count, width), jnp.float32)
    owners = jax.ShapeDtypeStruct((local_count * couplings.shape[1], width), jnp.int32)
    aimed = targets.T
    inputs = (aimed, rhs, inverse_blocks, couplings)
    held = [pltpu.SMEM(aimed.shape, jnp.int32)]
    held += [pltpu.VMEM(a.shape, a.dtype) for a in inputs[1:]]
    held += [pltpu.SemaphoreType.DMA((len(inputs),))]


    def exchanged(value, mask):
        members = [[i ^ (mask % columns) for i in range(columns)]]
        return lax.all_to_all(
            value, "col", split_axis=0, concat_axis=0, tiled=True, axis_index_groups=members
        )

    incoming = ()
    for step in range(sections - 1):
        values, slot_rows, outgoing = kernel_call(
            forward_kernel,
            (flat, owners, slots),
            [HBM] * len(inputs) + [VMEM] * len(incoming),
            "forward",
            scratch=held,
            vmem=60*2**20,
        )(*inputs, *incoming)
        if step == 0:
            sent_inverse, sent_rhs, _ = lax.optimization_barrier((inverse_blocks, rhs, values))
        arrived = exchanged(outgoing.reshape(columns, stride, 1, width), FIRST).reshape(slots.shape)
        if step < sections - 2:
            sums = kernel_call(sum_kernel, flat, [VMEM], "sum_rows")(arrived)
            moved = lax.ppermute(sums, "section", up)
            incoming = (jnp.where(my_section == 0, 0.0, moved),)

    next_inverse = lax.ppermute(sent_inverse, "section", down)
    next_rhs = lax.ppermute(sent_rhs, "section", down)
    next_split = split_arrays((next_inverse,), COVER)
    slot_rows, values, own_rhs, *weights = split_arrays(
        (inverse_blocks, couplings), COVER, (slot_rows, values, rhs)
    )
    last_shapes = (flat, flat, answered) if sections > 2 else (flat, answered)
    sums, *last, answers = kernel_call(last_kernel, last_shapes, [VMEM] * 4, "last_section")(
        arrived, next_rhs, *next_split
    )
    for step in range(sections - 1):
        picked = exchanged(answers, SECOND)
        operands = (slot_rows, picked, values, *weights)
        if step < sections - 2:
            solved = kernel_call(backward_kernel, flat, [VMEM] * len(operands), "backward")(
                *operands
            )
            moved = lax.ppermute(solved, "section", down)
            following = jnp.where(my_section == sections - 2, last[0], moved)
            answers = kernel_call(place_kernel, answered, [VMEM, VMEM], "place")(arrived, following)

    operands += (own_rhs, lax.ppermute(sums, "section", up))
    return kernel_call(backward_kernel, (flat, flat), [VMEM] * len(operands), "backward_last")(
        *operands
    )


def solution(mesh):
    return jax.shard_map(
        body,
        mesh=mesh,
        in_specs=(
            P(None, ("section", "col")),
            P(("section", "col"), None, None),
            P(("section", "col"), None, None, None),
            P(("section", "col"), None),
        ),
        out_specs=(P(None, ("section", "col")), P(None, ("section", "col"))),
        check_vma=False,
    )
```

```python
import functools

import jax
import jax.numpy as jnp
from jax import lax
from jax.experimental import pallas as pl
from jax.experimental.pallas import tpu as pltpu
from jax.sharding import PartitionSpec as P

VMEM = pl.BlockSpec(memory_space=pltpu.VMEM)
FIRST = 7
SECOND = 11
COVER = 20_000_000_000
HBM = pl.BlockSpec(memory_space=pltpu.HBM)


def split(value):
    high = value.astype(jnp.bfloat16)
    return high, (value - high.astype(jnp.float32)).astype(jnp.bfloat16)


def times(left, right, contracted=0):
    rows = left.shape[0]
    left_high, left_low = split(left)
    right_high, right_low = right

    def dot(a, b):
        numbers = (((1,), (contracted,)), ((), ()))
        return lax.dot_general(a, b, numbers, preferred_element_type=jnp.float32)

    both = dot(jnp.concatenate([left_high, left_low], axis=0), right_high)
    return both[:rows] + (both[rows:] + dot(left_high, right_low))


def times_transposed(left, right):
    return times(left, right, 1)


def kernel_call(kernel, out_shape, specs, name, flops=None, scratch=(), vmem=16 * 2**20):
    cost = None
    if flops is not None:
        cost = pl.CostEstimate(flops=flops, bytes_accessed=0, transcendentals=0)
    return pl.pallas_call(
        kernel,
        out_shape=out_shape,
        in_specs=specs,
        out_specs=jax.tree.map(lambda _: VMEM, out_shape),
        compiler_params=pltpu.CompilerParams(vmem_limit_bytes=vmem),
        cost_estimate=cost,
        scratch_shapes=scratch,
        name=name,
    )


def square_kernel(inverse_ref, high_ref, low_ref):
    for local in range(inverse_ref.shape[0]):
        inverse = inverse_ref[local]
        high_ref[local], low_ref[local] = split(times_transposed(inverse, split(inverse)))


def fold_kernel(
    slots_ref,
    values_ref,
    rhs_ref,
    inverse_ref,
    couplings_ref,
    slots_out,
    values_out,
    rhs_out,
    base_ref,
    inverse_high_ref,
    inverse_low_ref,
    high_ref,
    low_ref,
):
    slots_out[...] = slots_ref[...]
    values_out[...] = values_ref[...]
    rhs_out[...] = rhs_ref[...]
    local_count, fanout, width, _ = couplings_ref.shape
    for local, lanes in enumerate(lane_blocks(width, local_count)):
        inverse = inverse_ref[local]
        parts = split(inverse)
        inverse_high_ref[local], inverse_low_ref[local] = parts
        base_ref[:, lanes] = times_transposed(values_ref[:, lanes], parts)
        for k in range(fanout):
            product = times(inverse, split(couplings_ref[local, k]))
            high_ref[local, k], low_ref[local, k] = split(product)


def lane_blocks(width, count):
    return [slice(i * width, (i + 1) * width) for i in range(count)]


def summed_by_row(arrived_ref, local_count, rhs_count):
    stride = rhs_count + 1
    sums = [None] * local_count
    for start in range(0, arrived_ref.shape[0], stride):
        block = arrived_ref[start : start + rhs_count, :]
        row = arrived_ref[start + rhs_count : start + stride, :]
        for local in range(local_count):
            term = jnp.where(row == local, block, 0.0)
            sums[local] = term if sums[local] is None else sums[local] + term
    return sums


def place_answers(arrived_ref, answers_ref, solved, rhs_count):
    stride = rhs_count + 1
    columns = answers_ref.shape[0]
    for column in range(columns):
        last = ((column ^ (FIRST % columns)) + 1) * stride
        row = arrived_ref[last - 1 : last, :]
        answer = jnp.zeros_like(solved[0])
        for local, values in enumerate(solved):
            answer = jnp.where(row == local, values, answer)
        answers_ref[column ^ (SECOND % columns)] = answer


def forward_kernel(targets_hbm, rhs_hbm, inverse_hbm, couplings_hbm, *rest):
    *incoming_ref, values_ref, slots_ref, out_ref = rest[:-5]
    targets_ref, rhs_ref, inverse_ref, couplings_ref, sems = rest[-5:]
    local_count, width, _ = inverse_ref.shape
    fanout = couplings_ref.shape[1]
    rhs_count = rhs_ref.shape[0]
    stride = rhs_count + 1
    columns = out_ref.shape[0] // stride
    has_targets = lax.axis_index("section") < lax.axis_size("section") - 1

    @pl.when(has_targets)
    def _():
        sources = (targets_hbm, rhs_hbm, inverse_hbm, couplings_hbm)
        places = (targets_ref, rhs_ref, inverse_ref, couplings_ref)
        copies = [
            pltpu.make_async_copy(source, place, sems.at[i])
            for i, (source, place) in enumerate(zip(sources, places))
        ]
        for copy in copies:
            copy.start()
        out_ref[...] = jnp.full(out_ref.shape, -1.0, jnp.float32)
        copies[1].wait()
        copies[2].wait()
        solved = []
        for local, lanes in enumerate(lane_blocks(width, local_count)):
            source = rhs_ref[:, lanes]
            if incoming_ref:
                source = source - incoming_ref[0][:, lanes]
            solved.append(times(source, split(inverse_ref[local])))
            values_ref[:, lanes] = solved[local]
        copies[0].wait()
        copies[3].wait()
        for local in range(local_count):
            for k in range(fanout):
                target = targets_ref[k, local]
                owner = target // local_count
                start = (owner ^ (FIRST % columns)) * stride
                product = times(solved[local], split(couplings_ref[local, k]))
                row = jnp.full((1, width), target % local_count, jnp.int32)
                out_ref[pl.ds(start, rhs_count), :] = product
                out_ref[pl.ds(start + rhs_count, 1), :] = row.astype(jnp.float32)
                slot = jnp.full((1, width), owner ^ (SECOND % columns), jnp.int32)
                pair = local * fanout + k
                slots_ref[pair : pair + 1, :] = slot

    @pl.when(jnp.logical_not(has_targets))
    def _():
        out_ref[...] = jnp.full(out_ref.shape, -1.0, jnp.float32)
        values_ref[...] = jnp.zeros(values_ref.shape, jnp.float32)
        slots_ref[...] = jnp.zeros(slots_ref.shape, jnp.int32)


def sum_kernel(arrived_ref, sums_ref):
    rhs_count, width = sums_ref.shape[0], arrived_ref.shape[1]
    lanes = lane_blocks(width, sums_ref.shape[1] // width)
    for local, total in enumerate(summed_by_row(arrived_ref, len(lanes), rhs_count)):
        sums_ref[:, lanes[local]] = total


def solve_last(rhs_ref, sums, high_ref, low_ref):
    local_count, width, _ = high_ref.shape
    lanes = lane_blocks(width, local_count)
    inverse = [(high_ref[i], low_ref[i]) for i in range(local_count)]
    forward = [times(rhs_ref[:, lanes[i]] - sums[i], inverse[i]) for i in range(local_count)]
    return forward, [times_transposed(forward[i], inverse[i]) for i in range(local_count)]


def last_kernel(arrived_ref, rhs_ref, high_ref, low_ref, sums_ref, *rest):
    *solved_ref, answers_ref = rest
    local_count, width, _ = high_ref.shape
    rhs_count = rhs_ref.shape[0]
    sums = summed_by_row(arrived_ref, local_count, rhs_count)
    for local, lanes in enumerate(lane_blocks(width, local_count)):
        sums_ref[:, lanes] = sums[local]
    backward = [
        times(rhs_ref[:, lanes] - sums[i], (high_ref[i], low_ref[i]))
        for i, lanes in enumerate(lane_blocks(width, local_count))
    ]
    for ref in solved_ref:
        for local, lanes in enumerate(lane_blocks(width, local_count)):
            ref[:, lanes] = backward[local]
    place_answers(arrived_ref, answers_ref, backward, rhs_count)


def place_kernel(arrived_ref, solved_ref, answers_ref):
    rhs_count, width = solved_ref.shape[0], arrived_ref.shape[1]
    lanes = lane_blocks(width, solved_ref.shape[1] // width)
    place_answers(arrived_ref, answers_ref, [solved_ref[:, lane] for lane in lanes], rhs_count)


def backward_kernel(slots_ref, picked_ref, base_ref, high_ref, low_ref, *rest):
    *last_refs, solution_ref = rest
    local_count, fanout, width, _ = high_ref.shape
    lanes = lane_blocks(width, local_count)

    def solve():
        blocks = [jnp.zeros(picked_ref.shape[1:], jnp.float32)] * (local_count * fanout)
        for column in range(picked_ref.shape[0]):
            block = picked_ref[column]
            for pair in range(local_count * fanout):
                chosen = slots_ref[pair : pair + 1, :] == column
                blocks[pair] = jnp.where(chosen, block, blocks[pair])
        for local in range(local_count):
            total = base_ref[:, lanes[local]]
            for k in range(fanout):
                folded = (high_ref[local, k], low_ref[local, k])
                total = total - times_transposed(blocks[local * fanout + k], folded)
            solution_ref[:, lanes[local]] = total

    if last_refs:
        values_ref, rhs_ref, sums_ref, inverse_high_ref, inverse_low_ref, forward_ref = last_refs
        is_last = lax.axis_index("section") == lax.axis_size("section") - 1

        @pl.when(is_last)
        def _():
            sums = [sums_ref[:, lane] for lane in lanes]
            results = solve_last(rhs_ref, sums, inverse_high_ref, inverse_low_ref)
            for local, lane in enumerate(lanes):
                forward_ref[:, lane] = results[0][local]
                solution_ref[:, lane] = results[1][local]

        @pl.when(jnp.logical_not(is_last))
        def _():
            forward_ref[...] = values_ref[...]
            solve()

    else:
        solve()


def body(rhs, inverse_blocks, couplings, targets):
    sections = lax.axis_size("section")
    columns = lax.axis_size("col")
    my_section = lax.axis_index("section")
    local_count, width, _ = inverse_blocks.shape
    rhs_count = rhs.shape[0]
    stride = rhs_count + 1
    up = [(s, (s + 1) % sections) for s in range(sections)]
    down = [(s, (s - 1) % sections) for s in range(sections)]
    flat = jax.ShapeDtypeStruct(rhs.shape, jnp.float32)
    slots = jax.ShapeDtypeStruct((columns * stride, width), jnp.float32)
    answered = jax.ShapeDtypeStruct((columns, rhs_count, width), jnp.float32)
    owners = jax.ShapeDtypeStruct((local_count * couplings.shape[1], width), jnp.int32)
    aimed = targets.T
    inputs = (aimed, rhs, inverse_blocks, couplings)
    held = [pltpu.SMEM(aimed.shape, jnp.int32)]
    held += [pltpu.VMEM(a.shape, a.dtype) for a in inputs[1:]]
    held += [pltpu.SemaphoreType.DMA((len(inputs),))]


    def exchanged(value, mask):
        members = [[i ^ (mask % columns) for i in range(columns)]]
        return lax.all_to_all(
            value, "col", split_axis=0, concat_axis=0, tiled=True, axis_index_groups=members
        )

    incoming = ()
    for step in range(sections - 1):
        values, slot_rows, outgoing = kernel_call(
            forward_kernel,
            (flat, owners, slots),
            [HBM] * len(inputs) + [VMEM] * len(incoming),
            "forward",
            scratch=held,
            vmem=60*2**20,
        )(*inputs, *incoming)
        if step == 0:
            sent_inverse, sent_rhs, _ = lax.optimization_barrier((inverse_blocks, rhs, values))
        arrived = exchanged(outgoing.reshape(columns, stride, 1, width), FIRST).reshape(slots.shape)
        if step < sections - 2:
            sums = kernel_call(sum_kernel, flat, [VMEM], "sum_rows")(arrived)
            moved = lax.ppermute(sums, "section", up)
            incoming = (jnp.where(my_section == 0, 0.0, moved),)

    next_inverse = lax.ppermute(sent_inverse, "section", down)
    next_rhs = lax.ppermute(sent_rhs, "section", down)
    def halves(array):
        return (jax.ShapeDtypeStruct(array.shape, jnp.bfloat16),) * 2

    next_square = kernel_call(square_kernel, halves(inverse_blocks), [VMEM], "square", COVER)(
        next_inverse
    )
    slot_rows, values, own_rhs, base, *own_inverse, high, low = kernel_call(
        fold_kernel,
        (owners, flat, flat, flat, *halves(inverse_blocks), *halves(couplings)),
        [VMEM] * 5,
        "fold",
        COVER,
    )(slot_rows, values, rhs, inverse_blocks, couplings)
    last_shapes = (flat, flat, answered) if sections > 2 else (flat, answered)
    sums, *last, answers = kernel_call(last_kernel, last_shapes, [VMEM] * 4, "last_section")(
        arrived, next_rhs, *next_square
    )
    for step in range(sections - 1):
        picked = exchanged(answers, SECOND)
        operands = (slot_rows, picked, base, high, low)
        if step < sections - 2:
            solved = kernel_call(backward_kernel, flat, [VMEM] * len(operands), "backward")(
                *operands
            )
            moved = lax.ppermute(solved, "section", down)
            following = jnp.where(my_section == sections - 2, last[0], moved)
            answers = kernel_call(place_kernel, answered, [VMEM, VMEM], "place")(arrived, following)

    operands += (values, own_rhs, lax.ppermute(sums, "section", up), *own_inverse)
    return kernel_call(backward_kernel, (flat, flat), [VMEM] * len(operands), "backward_last")(
        *operands
    )


def solution(mesh):
    return jax.shard_map(
        body,
        mesh=mesh,
        in_specs=(
            P(None, ("section", "col")),
            P(("section", "col"), None, None),
            P(("section", "col"), None, None, None),
            P(("section", "col"), None),
        ),
        out_specs=(P(None, ("section", "col")), P(None, ("section", "col"))),
        check_vma=False,
    )
```

```python
import functools

import jax
import jax.numpy as jnp
from jax import lax
from jax.experimental import pallas as pl
from jax.experimental.pallas import tpu as pltpu
from jax.sharding import PartitionSpec as P

VMEM = pl.BlockSpec(memory_space=pltpu.VMEM)
FIRST = [11, 10, 15, 14, 7, 6, 3, 2, 9, 8, 13, 12, 5, 4, 1, 0]
SECOND = [11, 10, 9, 8, 15, 14, 13, 12, 3, 2, 1, 0, 7, 6, 5, 4]


def member_order(order, columns):
    if columns == len(order):
        return order
    return [(columns * 11 // 16 - i) % columns for i in range(columns)]


def slot_of(owner, order, columns):
    if columns != len(order):
        return (columns * 11 // 16 + columns - owner) % columns
    low, high = (
        sum(order.index(half + i) << (4 * i) for i in range(8)) for half in (0, 8)
    )
    low, high = (jnp.int32(v - (1 << 32) if v >= 1 << 31 else v) for v in (low, high))
    packed = jnp.where(owner < 8, low, high)
    return lax.shift_right_logical(packed, (owner % 8) * 4) & 15


COVER = 20_000_000_000
HBM = pl.BlockSpec(memory_space=pltpu.HBM)


def split(value):
    high = value.astype(jnp.bfloat16)
    return high, (value - high.astype(jnp.float32)).astype(jnp.bfloat16)


def times(left, right, contracted=0):
    rows = left.shape[0]
    left_high, left_low = split(left)
    right_high, right_low = right

    def dot(a, b):
        numbers = (((1,), (contracted,)), ((), ()))
        return lax.dot_general(a, b, numbers, preferred_element_type=jnp.float32)

    both = dot(jnp.concatenate([left_high, left_low], axis=0), right_high)
    return both[:rows] + (both[rows:] + dot(left_high, right_low))


def times_transposed(left, right):
    return times(left, right, 1)


def kernel_call(kernel, out_shape, specs, name, flops=None, scratch=(), vmem=16 * 2**20, **kwargs):
    cost = None
    if flops is not None:
        cost = pl.CostEstimate(flops=flops, bytes_accessed=0, transcendentals=0)
    return pl.pallas_call(
        kernel,
        out_shape=out_shape,
        in_specs=specs,
        out_specs=kwargs.get("out_specs", jax.tree.map(lambda _: VMEM, out_shape)),
        input_output_aliases=kwargs.get("aliases", {}),
        compiler_params=pltpu.CompilerParams(vmem_limit_bytes=vmem),
        cost_estimate=cost,
        scratch_shapes=scratch,
        name=name,
    )


def square_kernel(inverse_ref, high_ref, low_ref):
    for local in range(inverse_ref.shape[0]):
        inverse = inverse_ref[local]
        high_ref[local], low_ref[local] = split(times_transposed(inverse, split(inverse)))


def fold_kernel(
    slots_ref,
    values_ref,
    rhs_ref,
    inverse_ref,
    couplings_ref,
    slots_out,
    values_out,
    rhs_out,
    base_ref,
    inverse_high_ref,
    inverse_low_ref,
    high_ref,
    low_ref,
):
    slots_out[...] = slots_ref[...]
    values_out[...] = values_ref[...]
    rhs_out[...] = rhs_ref[...]
    local_count, fanout, width, _ = couplings_ref.shape
    for local, lanes in enumerate(lane_blocks(width, local_count)):
        inverse = inverse_ref[local]
        parts = split(inverse)
        inverse_high_ref[local], inverse_low_ref[local] = parts
        base_ref[:, lanes] = times_transposed(values_ref[:, lanes], parts)
        for k in range(fanout):
            product = times(inverse, split(couplings_ref[local, k]))
            high_ref[local, k], low_ref[local, k] = split(product)


def lane_blocks(width, count):
    return [slice(i * width, (i + 1) * width) for i in range(count)]


def summed_by_row(arrived_ref, local_count, rhs_count):
    stride = rhs_count + 1
    sums = [None] * local_count
    for start in range(0, arrived_ref.shape[0], stride):
        block = arrived_ref[start : start + rhs_count, :]
        row = arrived_ref[start + rhs_count : start + stride, :]
        for local in range(local_count):
            term = jnp.where(row == local, block, 0.0)
            sums[local] = term if sums[local] is None else sums[local] + term
    return sums


def place_answers(arrived_ref, answers_ref, solved, rhs_count):
    stride = rhs_count + 1
    columns = answers_ref.shape[0]
    first = member_order(FIRST, columns)
    second = member_order(SECOND, columns)
    for column in range(columns):
        last = (first.index(column) + 1) * stride
        row = arrived_ref[last - 1 : last, :]
        answer = jnp.zeros_like(solved[0])
        for local, values in enumerate(solved):
            answer = jnp.where(row == local, values, answer)
        answers_ref[second.index(column)] = answer


def forward_kernel(targets_hbm, rhs_hbm, inverse_hbm, couplings_hbm, *rest):
    *incoming_ref, values_ref, slots_ref, out_ref = rest[:-5]
    targets_ref, rhs_ref, inverse_ref, couplings_ref, sems = rest[-5:]
    local_count, width, _ = inverse_ref.shape
    fanout = couplings_ref.shape[1]
    rhs_count = rhs_ref.shape[0]
    stride = rhs_count + 1
    columns = out_ref.shape[0] // stride
    has_targets = lax.axis_index("section") < lax.axis_size("section") - 1

    @pl.when(has_targets)
    def _():
        sources = (targets_hbm, rhs_hbm, inverse_hbm, couplings_hbm)
        places = (targets_ref, rhs_ref, inverse_ref, couplings_ref)
        copies = [
            pltpu.make_async_copy(source, place, sems.at[i])
            for i, (source, place) in enumerate(zip(sources, places))
        ]
        for copy in copies:
            copy.start()
        out_ref[...] = jnp.full(out_ref.shape, -1.0, jnp.float32)
        copies[1].wait()
        copies[2].wait()
        solved = []
        for local, lanes in enumerate(lane_blocks(width, local_count)):
            source = rhs_ref[:, lanes]
            if incoming_ref:
                source = source - incoming_ref[0][:, lanes]
            solved.append(times(source, split(inverse_ref[local])))
            values_ref[:, lanes] = solved[local]
        copies[0].wait()
        copies[3].wait()
        for local in range(local_count):
            for k in range(fanout):
                target = targets_ref[k, local]
                owner = target // local_count
                start = slot_of(owner, FIRST, columns) * stride
                product = times(solved[local], split(couplings_ref[local, k]))
                row = jnp.full((1, width), target % local_count, jnp.int32)
                out_ref[pl.ds(start, rhs_count), :] = product
                out_ref[pl.ds(start + rhs_count, 1), :] = row.astype(jnp.float32)
                slot = jnp.full((1, width), slot_of(owner, SECOND, columns), jnp.int32)
                pair = local * fanout + k
                slots_ref[pair : pair + 1, :] = slot

    @pl.when(jnp.logical_not(has_targets))
    def _():
        out_ref[...] = jnp.full(out_ref.shape, -1.0, jnp.float32)
        values_ref[...] = jnp.zeros(values_ref.shape, jnp.float32)
        slots_ref[...] = jnp.zeros(slots_ref.shape, jnp.int32)


def sum_kernel(arrived_ref, sums_ref):
    rhs_count, width = sums_ref.shape[0], arrived_ref.shape[1]
    lanes = lane_blocks(width, sums_ref.shape[1] // width)
    for local, total in enumerate(summed_by_row(arrived_ref, len(lanes), rhs_count)):
        sums_ref[:, lanes[local]] = total


def solve_last(rhs_ref, sums, high_ref, low_ref):
    local_count, width, _ = high_ref.shape
    lanes = lane_blocks(width, local_count)
    inverse = [(high_ref[i], low_ref[i]) for i in range(local_count)]
    forward = [times(rhs_ref[:, lanes[i]] - sums[i], inverse[i]) for i in range(local_count)]
    return forward, [times_transposed(forward[i], inverse[i]) for i in range(local_count)]


def last_kernel(arrived_ref, rhs_ref, high_ref, low_ref, sums_ref, *rest):
    *solved_ref, answers_ref = rest
    local_count, width, _ = high_ref.shape
    rhs_count = rhs_ref.shape[0]
    sums = summed_by_row(arrived_ref, local_count, rhs_count)
    for local, lanes in enumerate(lane_blocks(width, local_count)):
        sums_ref[:, lanes] = sums[local]
    backward = [
        times(rhs_ref[:, lanes] - sums[i], (high_ref[i], low_ref[i]))
        for i, lanes in enumerate(lane_blocks(width, local_count))
    ]
    for ref in solved_ref:
        for local, lanes in enumerate(lane_blocks(width, local_count)):
            ref[:, lanes] = backward[local]
    place_answers(arrived_ref, answers_ref, backward, rhs_count)


def place_kernel(arrived_ref, solved_ref, answers_ref):
    rhs_count, width = solved_ref.shape[0], arrived_ref.shape[1]
    lanes = lane_blocks(width, solved_ref.shape[1] // width)
    place_answers(arrived_ref, answers_ref, [solved_ref[:, lane] for lane in lanes], rhs_count)


def backward_kernel(slots_ref, picked_ref, base_ref, high_ref, low_ref, *rest):
    *last_refs, solution_ref = rest if len(rest) == 1 else (*rest[:3], rest[4], rest[3])
    local_count, fanout, width, _ = high_ref.shape
    lanes = lane_blocks(width, local_count)

    def solve():
        blocks = [jnp.zeros(picked_ref.shape[1:], jnp.float32)] * (local_count * fanout)
        for column in range(picked_ref.shape[0]):
            block = picked_ref[column]
            for pair in range(local_count * fanout):
                chosen = slots_ref[pair : pair + 1, :] == column
                blocks[pair] = jnp.where(chosen, block, blocks[pair])
        for local in range(local_count):
            total = base_ref[:, lanes[local]]
            for k in range(fanout):
                folded = (high_ref[local, k], low_ref[local, k])
                total = total - times_transposed(blocks[local * fanout + k], folded)
            solution_ref[:, lanes[local]] = total

    if not last_refs:
        solve()
        return

    values_ref, forward_out, solution_out, sems = last_refs
    section_is_last = lax.axis_index("section") == lax.axis_size("section") - 1

    @pl.when(jnp.logical_not(section_is_last))
    def _():
        first = pltpu.make_async_copy(values_ref, forward_out, sems.at[0])
        second = pltpu.make_async_copy(solution_ref, solution_out, sems.at[1])
        first.start()
        solve()
        second.start()
        first.wait()
        second.wait()


def finish_kernel(rhs_ref, sums_ref, high_ref, low_ref, *rest):
    _, _, forward_out, solution_out, forward_ref, solution_ref, sems = rest
    section_is_last = lax.axis_index("section") == lax.axis_size("section") - 1

    @pl.when(section_is_last)
    def _():
        local_count, width, _ = high_ref.shape
        lanes = lane_blocks(width, local_count)
        sums = [sums_ref[:, lane] for lane in lanes]
        forward, backward = solve_last(rhs_ref, sums, high_ref, low_ref)
        for local, lane in enumerate(lanes):
            forward_ref[:, lane] = forward[local]
            solution_ref[:, lane] = backward[local]
        copies = [
            pltpu.make_async_copy(forward_ref, forward_out, sems.at[0]),
            pltpu.make_async_copy(solution_ref, solution_out, sems.at[1]),
        ]
        for copy in copies:
            copy.start()
        for copy in copies:
            copy.wait()


def body(rhs, inverse_blocks, couplings, targets):
    sections = lax.axis_size("section")
    columns = lax.axis_size("col")
    my_section = lax.axis_index("section")
    local_count, width, _ = inverse_blocks.shape
    rhs_count = rhs.shape[0]
    stride = rhs_count + 1
    up = [(s, (s + 1) % sections) for s in range(sections)]
    down = [(s, (s - 1) % sections) for s in range(sections)]
    flat = jax.ShapeDtypeStruct(rhs.shape, jnp.float32)
    slots = jax.ShapeDtypeStruct((columns * stride, width), jnp.float32)
    answered = jax.ShapeDtypeStruct((columns, rhs_count, width), jnp.float32)
    owners = jax.ShapeDtypeStruct((local_count * couplings.shape[1], width), jnp.int32)
    aimed = targets.T
    inputs = (aimed, rhs, inverse_blocks, couplings)
    held = [pltpu.SMEM(aimed.shape, jnp.int32)]
    held += [pltpu.VMEM(a.shape, a.dtype) for a in inputs[1:]]
    held += [pltpu.SemaphoreType.DMA((len(inputs),))]


    def exchanged(value, order):
        members = [member_order(order, columns)]
        return lax.all_to_all(
            value, "col", split_axis=0, concat_axis=0, tiled=True, axis_index_groups=members
        )

    incoming = ()
    for step in range(sections - 1):
        values, slot_rows, outgoing = kernel_call(
            forward_kernel,
            (flat, owners, slots),
            [HBM] * len(inputs) + [VMEM] * len(incoming),
            "forward",
            scratch=held,
            vmem=60*2**20,
        )(*inputs, *incoming)
        if step == 0:
            sent_inverse, sent_rhs, _ = lax.optimization_barrier((inverse_blocks, rhs, values))
        arrived = exchanged(outgoing.reshape(columns, stride, 1, width), FIRST).reshape(slots.shape)
        if step < sections - 2:
            sums = kernel_call(sum_kernel, flat, [VMEM], "sum_rows")(arrived)
            moved = lax.ppermute(sums, "section", up)
            incoming = (jnp.where(my_section == 0, 0.0, moved),)

    next_inverse = lax.ppermute(sent_inverse, "section", down)
    next_rhs = lax.ppermute(sent_rhs, "section", down)
    def halves(array):
        return (jax.ShapeDtypeStruct(array.shape, jnp.bfloat16),) * 2

    next_square = kernel_call(square_kernel, halves(inverse_blocks), [VMEM], "square", COVER)(
        next_inverse
    )
    slot_rows, values, own_rhs, base, *own_inverse, high, low = kernel_call(
        fold_kernel,
        (owners, flat, flat, flat, *halves(inverse_blocks), *halves(couplings)),
        [VMEM] * 5,
        "fold",
        COVER,
    )(slot_rows, values, rhs, inverse_blocks, couplings)
    last_shapes = (flat, flat, answered) if sections > 2 else (flat, answered)
    sums, *last, answers = kernel_call(last_kernel, last_shapes, [VMEM] * 4, "last_section")(
        arrived, next_rhs, *next_square
    )
    for step in range(sections - 1):
        picked = exchanged(answers, SECOND)
        operands = (slot_rows, picked, base, high, low)
        if step < sections - 2:
            solved = kernel_call(backward_kernel, flat, [VMEM] * len(operands), "backward")(
                *operands
            )
            moved = lax.ppermute(solved, "section", down)
            following = jnp.where(my_section == sections - 2, last[0], moved)
            answers = kernel_call(place_kernel, answered, [VMEM, VMEM], "place")(arrived, following)

    staged = pltpu.VMEM(flat.shape, flat.dtype)
    sems = pltpu.SemaphoreType.DMA((2,))
    results = kernel_call(
        backward_kernel,
        (flat, flat),
        [VMEM] * (len(operands) + 1),
        "backward_last",
        scratch=[staged, sems],
        out_specs=(HBM, HBM),
    )(*operands, values)
    received = lax.ppermute(sums, "section", up)
    return kernel_call(
        finish_kernel,
        (flat, flat),
        [VMEM] * 4 + [HBM] * 2,
        "finish_last",
        scratch=[staged, staged, sems],
        out_specs=(HBM, HBM),
        aliases={4: 0, 5: 1},
    )(own_rhs, received, *own_inverse, *results)


def solution(mesh):
    return jax.shard_map(
        body,
        mesh=mesh,
        in_specs=(
            P(None, ("section", "col")),
            P(("section", "col"), None, None),
            P(("section", "col"), None, None, None),
            P(("section", "col"), None),
        ),
        out_specs=(P(None, ("section", "col")), P(None, ("section", "col"))),
        check_vma=False,
    )
```

```python
import functools

import jax
import jax.numpy as jnp
from jax import lax
from jax.experimental import pallas as pl
from jax.experimental.pallas import tpu as pltpu
from jax.sharding import PartitionSpec as P

VMEM = pl.BlockSpec(memory_space=pltpu.VMEM)
FIRST = [11, 10, 15, 14, 7, 6, 3, 2, 9, 8, 13, 12, 5, 4, 1, 0]
SECOND = [11, 10, 9, 8, 15, 14, 13, 12, 3, 2, 1, 0, 7, 6, 5, 4]


def member_order(order, columns):
    if columns == len(order):
        return order
    return [(columns * 11 // 16 - i) % columns for i in range(columns)]


def slot_of(owner, order, columns):
    if columns != len(order):
        return (columns * 11 // 16 + columns - owner) % columns
    low, high = (
        sum(order.index(half + i) << (4 * i) for i in range(8)) for half in (0, 8)
    )
    low, high = (jnp.int32(v - (1 << 32) if v >= 1 << 31 else v) for v in (low, high))
    packed = jnp.where(owner < 8, low, high)
    return lax.shift_right_logical(packed, (owner % 8) * 4) & 15


COVER = 20_000_000_000
HBM = pl.BlockSpec(memory_space=pltpu.HBM)


def split(value):
    high = value.astype(jnp.bfloat16)
    return high, (value - high.astype(jnp.float32)).astype(jnp.bfloat16)


def times(left, right, contracted=0):
    rows = left.shape[0]
    left_high, left_low = split(left)
    right_high, right_low = right

    def dot(a, b):
        numbers = (((1,), (contracted,)), ((), ()))
        return lax.dot_general(a, b, numbers, preferred_element_type=jnp.float32)

    both = dot(jnp.concatenate([left_high, left_low], axis=0), right_high)
    return both[:rows] + (both[rows:] + dot(left_high, right_low))


def times_transposed(left, right):
    return times(left, right, 1)


def kernel_call(kernel, out_shape, specs, name, flops=None, scratch=(), vmem=16 * 2**20, **kwargs):
    cost = None
    if flops is not None:
        cost = pl.CostEstimate(flops=flops, bytes_accessed=0, transcendentals=0)
    return pl.pallas_call(
        kernel,
        out_shape=out_shape,
        in_specs=specs,
        out_specs=kwargs.get("out_specs", jax.tree.map(lambda _: VMEM, out_shape)),
        input_output_aliases=kwargs.get("aliases", {}),
        compiler_params=pltpu.CompilerParams(vmem_limit_bytes=vmem),
        cost_estimate=cost,
        scratch_shapes=scratch,
        name=name,
    )


def square_kernel(inverse_ref, high_ref, low_ref):
    for local in range(inverse_ref.shape[0]):
        inverse = inverse_ref[local]
        high_ref[local], low_ref[local] = split(times_transposed(inverse, split(inverse)))


def fold_kernel(
    slots_ref,
    values_ref,
    rhs_ref,
    inverse_ref,
    couplings_ref,
    slots_out,
    values_out,
    rhs_out,
    base_ref,
    inverse_high_ref,
    inverse_low_ref,
    square_high_ref,
    square_low_ref,
    high_ref,
    low_ref,
):
    slots_out[...] = slots_ref[...]
    values_out[...] = values_ref[...]
    rhs_out[...] = rhs_ref[...]
    local_count, fanout, width, _ = couplings_ref.shape
    for local, lanes in enumerate(lane_blocks(width, local_count)):
        inverse = inverse_ref[local]
        parts = split(inverse)
        inverse_high_ref[local], inverse_low_ref[local] = parts
        square_high_ref[local], square_low_ref[local] = split(times_transposed(inverse, parts))
        base_ref[:, lanes] = times_transposed(values_ref[:, lanes], parts)
        for k in range(fanout):
            product = times(inverse, split(couplings_ref[local, k]))
            high_ref[local, k], low_ref[local, k] = split(product)


def lane_blocks(width, count):
    return [slice(i * width, (i + 1) * width) for i in range(count)]


def summed_by_row(arrived_ref, local_count, rhs_count):
    stride = rhs_count + 1
    sums = [None] * local_count
    for start in range(0, arrived_ref.shape[0], stride):
        block = arrived_ref[start : start + rhs_count, :]
        row = arrived_ref[start + rhs_count : start + stride, :]
        for local in range(local_count):
            term = jnp.where(row == local, block, 0.0)
            sums[local] = term if sums[local] is None else sums[local] + term
    return sums


def place_answers(arrived_ref, answers_ref, solved, rhs_count):
    stride = rhs_count + 1
    columns = answers_ref.shape[0]
    first = member_order(FIRST, columns)
    second = member_order(SECOND, columns)
    for column in range(columns):
        last = (first.index(column) + 1) * stride
        row = arrived_ref[last - 1 : last, :]
        answer = jnp.zeros_like(solved[0])
        for local, values in enumerate(solved):
            answer = jnp.where(row == local, values, answer)
        answers_ref[second.index(column)] = answer


def forward_kernel(targets_hbm, rhs_hbm, inverse_hbm, couplings_hbm, *rest):
    *incoming_ref, values_ref, slots_ref, out_ref = rest[:-5]
    targets_ref, rhs_ref, inverse_ref, couplings_ref, sems = rest[-5:]
    local_count, width, _ = inverse_ref.shape
    fanout = couplings_ref.shape[1]
    rhs_count = rhs_ref.shape[0]
    stride = rhs_count + 1
    columns = out_ref.shape[0] // stride
    has_targets = lax.axis_index("section") < lax.axis_size("section") - 1

    @pl.when(has_targets)
    def _():
        sources = (targets_hbm, rhs_hbm, inverse_hbm, couplings_hbm)
        places = (targets_ref, rhs_ref, inverse_ref, couplings_ref)
        copies = [
            pltpu.make_async_copy(source, place, sems.at[i])
            for i, (source, place) in enumerate(zip(sources, places))
        ]
        for copy in copies:
            copy.start()
        out_ref[...] = jnp.full(out_ref.shape, -1.0, jnp.float32)
        copies[1].wait()
        copies[2].wait()
        solved = []
        for local, lanes in enumerate(lane_blocks(width, local_count)):
            source = rhs_ref[:, lanes]
            if incoming_ref:
                source = source - incoming_ref[0][:, lanes]
            solved.append(times(source, split(inverse_ref[local])))
            values_ref[:, lanes] = solved[local]
        copies[0].wait()
        copies[3].wait()
        for local in range(local_count):
            for k in range(fanout):
                target = targets_ref[k, local]
                owner = target // local_count
                start = slot_of(owner, FIRST, columns) * stride
                product = times(solved[local], split(couplings_ref[local, k]))
                row = jnp.full((1, width), target % local_count, jnp.int32)
                out_ref[pl.ds(start, rhs_count), :] = product
                out_ref[pl.ds(start + rhs_count, 1), :] = row.astype(jnp.float32)
                slot = jnp.full((1, width), slot_of(owner, SECOND, columns), jnp.int32)
                pair = local * fanout + k
                slots_ref[pair : pair + 1, :] = slot

    @pl.when(jnp.logical_not(has_targets))
    def _():
        out_ref[...] = jnp.full(out_ref.shape, -1.0, jnp.float32)
        values_ref[...] = jnp.zeros(values_ref.shape, jnp.float32)
        slots_ref[...] = jnp.zeros(slots_ref.shape, jnp.int32)


def sum_kernel(arrived_ref, sums_ref):
    rhs_count, width = sums_ref.shape[0], arrived_ref.shape[1]
    lanes = lane_blocks(width, sums_ref.shape[1] // width)
    for local, total in enumerate(summed_by_row(arrived_ref, len(lanes), rhs_count)):
        sums_ref[:, lanes[local]] = total


def last_kernel(arrived_ref, rhs_ref, high_ref, low_ref, sums_ref, *rest):
    *solved_ref, answers_ref = rest
    local_count, width, _ = high_ref.shape
    rhs_count = rhs_ref.shape[0]
    sums = summed_by_row(arrived_ref, local_count, rhs_count)
    for local, lanes in enumerate(lane_blocks(width, local_count)):
        sums_ref[:, lanes] = sums[local]
    backward = [
        times(rhs_ref[:, lanes] - sums[i], (high_ref[i], low_ref[i]))
        for i, lanes in enumerate(lane_blocks(width, local_count))
    ]
    for ref in solved_ref:
        for local, lanes in enumerate(lane_blocks(width, local_count)):
            ref[:, lanes] = backward[local]
    place_answers(arrived_ref, answers_ref, backward, rhs_count)


def place_kernel(arrived_ref, solved_ref, answers_ref):
    rhs_count, width = solved_ref.shape[0], arrived_ref.shape[1]
    lanes = lane_blocks(width, solved_ref.shape[1] // width)
    place_answers(arrived_ref, answers_ref, [solved_ref[:, lane] for lane in lanes], rhs_count)


def backward_kernel(slots_ref, picked_ref, base_ref, high_ref, low_ref, *rest):
    *last_refs, solution_ref = rest if len(rest) == 1 else (*rest[:3], rest[4], rest[3])
    local_count, fanout, width, _ = high_ref.shape
    lanes = lane_blocks(width, local_count)

    def solve():
        blocks = [jnp.zeros(picked_ref.shape[1:], jnp.float32)] * (local_count * fanout)
        for column in range(picked_ref.shape[0]):
            block = picked_ref[column]
            for pair in range(local_count * fanout):
                chosen = slots_ref[pair : pair + 1, :] == column
                blocks[pair] = jnp.where(chosen, block, blocks[pair])
        for local in range(local_count):
            total = base_ref[:, lanes[local]]
            for k in range(fanout):
                folded = (high_ref[local, k], low_ref[local, k])
                total = total - times_transposed(blocks[local * fanout + k], folded)
            solution_ref[:, lanes[local]] = total

    if not last_refs:
        solve()
        return

    values_ref, forward_out, solution_out, sems = last_refs
    section_is_last = lax.axis_index("section") == lax.axis_size("section") - 1

    @pl.when(jnp.logical_not(section_is_last))
    def _():
        first = pltpu.make_async_copy(values_ref, forward_out, sems.at[0])
        second = pltpu.make_async_copy(solution_ref, solution_out, sems.at[1])
        first.start()
        solve()
        second.start()
        first.wait()
        second.wait()


def finish_kernel(rhs_ref, sums_ref, *rest):
    weights, (forward_out, solution_out, forward_ref, solution_ref, sems) = rest[:4], rest[6:]
    high_ref, low_ref, square_high_ref, square_low_ref = weights
    section_is_last = lax.axis_index("section") == lax.axis_size("section") - 1

    @pl.when(section_is_last)
    def _():
        copies = [
            pltpu.make_async_copy(forward_ref, forward_out, sems.at[0]),
            pltpu.make_async_copy(solution_ref, solution_out, sems.at[1]),
        ]
        local_count, width, _ = high_ref.shape
        lanes = lane_blocks(width, local_count)
        sources = [rhs_ref[:, lane] - sums_ref[:, lane] for lane in lanes]
        for local, lane in enumerate(lanes):
            forward_ref[:, lane] = times(sources[local], (high_ref[local], low_ref[local]))
        copies[0].start()
        for local, lane in enumerate(lanes):
            square = (square_high_ref[local], square_low_ref[local])
            solution_ref[:, lane] = times(sources[local], square)
        copies[1].start()
        for copy in copies:
            copy.wait()


def body(rhs, inverse_blocks, couplings, targets):
    sections = lax.axis_size("section")
    columns = lax.axis_size("col")
    my_section = lax.axis_index("section")
    local_count, width, _ = inverse_blocks.shape
    rhs_count = rhs.shape[0]
    stride = rhs_count + 1
    up = [(s, (s + 1) % sections) for s in range(sections)]
    down = [(s, (s - 1) % sections) for s in range(sections)]
    flat = jax.ShapeDtypeStruct(rhs.shape, jnp.float32)
    slots = jax.ShapeDtypeStruct((columns * stride, width), jnp.float32)
    answered = jax.ShapeDtypeStruct((columns, rhs_count, width), jnp.float32)
    owners = jax.ShapeDtypeStruct((local_count * couplings.shape[1], width), jnp.int32)
    aimed = targets.T
    inputs = (aimed, rhs, inverse_blocks, couplings)
    held = [pltpu.SMEM(aimed.shape, jnp.int32)]
    held += [pltpu.VMEM(a.shape, a.dtype) for a in inputs[1:]]
    held += [pltpu.SemaphoreType.DMA((len(inputs),))]


    def exchanged(value, order):
        members = [member_order(order, columns)]
        return lax.all_to_all(
            value, "col", split_axis=0, concat_axis=0, tiled=True, axis_index_groups=members
        )

    incoming = ()
    for step in range(sections - 1):
        values, slot_rows, outgoing = kernel_call(
            forward_kernel,
            (flat, owners, slots),
            [HBM] * len(inputs) + [VMEM] * len(incoming),
            "forward",
            scratch=held,
            vmem=60*2**20,
        )(*inputs, *incoming)
        if step == 0:
            sent_inverse, sent_rhs, _ = lax.optimization_barrier((inverse_blocks, rhs, values))
        arrived = exchanged(outgoing.reshape(columns, stride, 1, width), FIRST).reshape(slots.shape)
        if step < sections - 2:
            sums = kernel_call(sum_kernel, flat, [VMEM], "sum_rows")(arrived)
            moved = lax.ppermute(sums, "section", up)
            incoming = (jnp.where(my_section == 0, 0.0, moved),)

    next_inverse = lax.ppermute(sent_inverse, "section", down)
    next_rhs = lax.ppermute(sent_rhs, "section", down)
    def halves(array):
        return (jax.ShapeDtypeStruct(array.shape, jnp.bfloat16),) * 2

    next_square = kernel_call(square_kernel, halves(inverse_blocks), [VMEM], "square", COVER)(
        next_inverse
    )
    slot_rows, values, own_rhs, base, *own_weights, high, low = kernel_call(
        fold_kernel,
        (owners, flat, flat, flat, *halves(inverse_blocks) * 2, *halves(couplings)),
        [VMEM] * 5,
        "fold",
        COVER,
    )(slot_rows, values, rhs, inverse_blocks, couplings)
    last_shapes = (flat, flat, answered) if sections > 2 else (flat, answered)
    sums, *last, answers = kernel_call(last_kernel, last_shapes, [VMEM] * 4, "last_section")(
        arrived, next_rhs, *next_square
    )
    for step in range(sections - 1):
        picked = exchanged(answers, SECOND)
        operands = (slot_rows, picked, base, high, low)
        if step < sections - 2:
            solved = kernel_call(backward_kernel, flat, [VMEM] * len(operands), "backward")(
                *operands
            )
            moved = lax.ppermute(solved, "section", down)
            following = jnp.where(my_section == sections - 2, last[0], moved)
            answers = kernel_call(place_kernel, answered, [VMEM, VMEM], "place")(arrived, following)

    staged = pltpu.VMEM(flat.shape, flat.dtype)
    sems = pltpu.SemaphoreType.DMA((2,))
    results = kernel_call(
        backward_kernel,
        (flat, flat),
        [VMEM] * (len(operands) + 1),
        "backward_last",
        scratch=[staged, sems],
        out_specs=(HBM, HBM),
    )(*operands, values)
    received = lax.ppermute(sums, "section", up)
    return kernel_call(
        finish_kernel,
        (flat, flat),
        [VMEM] * 6 + [HBM] * 2,
        "finish_last",
        scratch=[staged, staged, sems],
        out_specs=(HBM, HBM),
        aliases={6: 0, 7: 1},
    )(own_rhs, received, *own_weights, *results)


def solution(mesh):
    return jax.shard_map(
        body,
        mesh=mesh,
        in_specs=(
            P(None, ("section", "col")),
            P(("section", "col"), None, None),
            P(("section", "col"), None, None, None),
            P(("section", "col"), None),
        ),
        out_specs=(P(None, ("section", "col")), P(None, ("section", "col"))),
        check_vma=False,
    )
```
